256 devices in a mesh: inst: 64 (over z, x, y_hi), tp: 4 (over y_lo, core).
Axes of the slice: x: 4, y: 4 (y_hi: 2, y_lo: 2; y = y_hi * 2 + y_lo), z: 8, core: 2. Of those that a mesh axis runs over, the one named last changes fastest.
Arguments:
- x_first: bfloat16 [1024, 8192], P('inst', 'tp'), may hold values from -6 to 6
- x_second: bfloat16 [1024, 8192], P('inst', 'tp'), may hold values from -6 to 6
- w_kv: bfloat16 [8192, 1024], P('tp'), may hold values from -0.0625 to 0.0625
- q_first: bfloat16 [1024, 4096], P('inst', 'tp'), may hold values from -24 to 24
- q_second: bfloat16 [1024, 4096], P('inst', 'tp'), may hold values from -24 to 24
- kv_cache: bfloat16 [32768, 16, 1024], P('inst', None, 'tp'), may hold values from -24 to 24
- page_table: int32 [1024, 32], P('inst'), may hold values from 0 to 511, as said below
- lengths: int32 [1024], replicated, may hold values from 1 to 510, as said below
- mig_req: int32 [64, 8], replicated, may hold values from 0 to 15, as said below
Outputs:
- attn_first: bfloat16 [1024, 4096], P('inst', 'tp')
- attn_second: bfloat16 [1024, 4096], P('inst', 'tp')
- imported: bfloat16 [512, 512, 1024], P('inst', None, 'tp')
The draws below stay inside these ranges and needn't reach their ends.
Inputs may be any that keep to these rules, and one draw needn't show every extreme that they name: `page_table`: within one instance's 16 rows each page of 0 to 511 appears exactly once. `lengths`: both new tokens fit within 512 positions. `mig_req`: row p lists 8 distinct requests of instance p.
All inputs are finite; a program needn't handle non-finite values.
Results may differ from the reference program's by a relative error of at most 0.005.
Values may be sent and summed in bfloat16 or wider, within the bound.
No kernel may reach another device: no remote copies, remote signals or barrier semaphores. Data moves between devices by JAX's collectives and lax.ppermute only.
A program may use at most 64 MiB of HBM per device.

```python
import jax
import jax.numpy as jnp
from jax import lax

D = 8192
HD = 128
QH = 32
KVH = 4
PAGE = 16
REQ = 16
MAXP = 32
MIG = 8
CTX = 512
POOL = 512
NREQ = 1024
NPOOL = 32768
NMIG = 512
N_INST = 64


def query_draw(key, salt_value):
    key = jax.random.fold_in(key, salt_value)
    noise_key = jax.random.fold_in(key, 0)
    values = jnp.clip(jax.random.normal(noise_key, (NREQ, KVH, QH // KVH, HD), jnp.float32), -4.0, 4.0)
    return values.reshape(NREQ, QH * HD).astype(jnp.bfloat16)


def draw_q_first(key, part):
    return query_draw(key, 11)


def draw_q_second(key, part):
    return query_draw(key, 12)


def draw_kv_cache(key, part):
    key = jax.random.fold_in(key, 3)
    noise_key = jax.random.fold_in(key, 0)
    values = jnp.clip(jax.random.normal(noise_key, (NPOOL, PAGE, KVH, 2, HD), jnp.float32), -4.0, 4.0)
    return values.reshape(NPOOL, PAGE, 2 * KVH * HD).astype(jnp.bfloat16)


def draw_page_table(key, part):
    key = jax.random.fold_in(key, 5)
    instance_keys = jax.random.split(key, N_INST)
    orders = jax.vmap(lambda one_key: jax.random.permutation(one_key, POOL))(instance_keys)
    return orders.reshape(NREQ, MAXP).astype(jnp.int32)


def draw_lengths(key, part):
    key = jax.random.fold_in(key, 6)
    ceiling_key, raw_key, long_key, short_key = jax.random.split(key, 4)
    ceilings = jax.random.randint(ceiling_key, (N_INST, 1), CTX // 2, CTX - 1)
    lower_half = ceilings // 2
    raw_draw = jax.random.randint(raw_key, (N_INST, REQ), 0, 1 << 20)
    drawn_len = (1 + lower_half + raw_draw % (ceilings - lower_half)).reshape(NREQ).astype(jnp.int32)
    longest = jax.random.randint(long_key, (), 0, NREQ)
    shortest = (longest + 1 + jax.random.randint(short_key, (), 0, NREQ - 1)) % NREQ
    drawn_len = drawn_len.at[longest].set(CTX - 2)
    drawn_len = drawn_len.at[shortest].set(1)
    return drawn_len.astype(jnp.int32)


def draw_mig_req(key, part):
    key = jax.random.fold_in(key, 9)
    order_key, pick_key = jax.random.split(key)
    instance_keys = jax.random.split(order_key, N_INST)
    orders = jax.vmap(lambda one_key: jax.random.permutation(one_key, REQ))(instance_keys)[:, :MIG]
    special = jnp.concatenate([jnp.full((1,), REQ - 1, jnp.int32), jnp.arange(MIG - 1, dtype=jnp.int32)])
    chosen_row = jax.random.randint(pick_key, (), 0, N_INST)
    row_index = jnp.arange(N_INST)[:, None]
    return jnp.where(row_index == chosen_row, special[None, :], orders.astype(jnp.int32)).astype(jnp.int32)


def level_of(stream_key, extent, pieces, low, top_value):
    def one(dim, shards_of):
        heights = jax.random.uniform(jax.random.fold_in(jax.random.fold_in(stream_key, 6), dim), (shards_of,), jnp.float32, low / len(pieces), top_value / len(pieces))
        return jnp.repeat(jnp.exp(heights), extent[dim] // shards_of).reshape((-1,) + (1,) * (len(extent) - dim - 1))

    loudness = one(*pieces[0])
    for cut in pieces[1:]:
        loudness = loudness * one(*cut)
    return loudness


def centred(stream_key, extent, width, most, cuts=(), kind=jnp.bfloat16):
    gain = level_of(stream_key, extent, cuts, -0.22, 0.18) if cuts else 1.0
    result = jax.random.normal(stream_key, extent, jnp.float32) * width * gain
    return jnp.minimum(jnp.maximum(result, -most), most).astype(kind)


def setup_inputs(seed: int = 0) -> dict:
    key_list = jax.random.split(jax.random.key(seed), 10)
    x_first = centred(key_list[0], (NREQ, D), 1.0, 6.0, ((0, 64), (1, 4)))
    x_second = centred(key_list[1], (NREQ, D), 1.0, 6.0, ((0, 64), (1, 4)))
    w_kv = centred(key_list[2], (D, 2 * KVH * HD), D ** -0.5, 0.0625, ((0, 4),))
    q_first = draw_q_first(jax.random.fold_in(key_list[9], 71), 0)
    q_second = draw_q_second(jax.random.fold_in(key_list[9], 71), 0)
    kv_cache = draw_kv_cache(jax.random.fold_in(key_list[9], 71), 0)
    page_table = draw_page_table(jax.random.fold_in(key_list[9], 71), 0)
    lengths = draw_lengths(jax.random.fold_in(key_list[9], 71), 0)
    mig_req = draw_mig_req(jax.random.fold_in(key_list[9], 71), 0)
    return dict(x_first=x_first, x_second=x_second, w_kv=w_kv, q_first=q_first, q_second=q_second, kv_cache=kv_cache, page_table=page_table, lengths=lengths, mig_req=mig_req)


def insert_rows(tokens, new_rows, place_at):
    positions = jnp.arange(CTX, dtype=jnp.int32)
    hit_mask = positions[None, :] == place_at[:, None]
    return jnp.where(hit_mask[:, :, None], new_rows[:, None, :], tokens)


def softmax_read(asked_rows, tokens, last_live):
    shaped = tokens.reshape(REQ, CTX, KVH, 2, HD)
    key_part = shaped[:, :, :, 0, :].astype(jnp.float32)
    value_part = shaped[:, :, :, 1, :].astype(jnp.float32)
    asked = asked_rows.astype(jnp.float32).reshape(REQ, KVH, QH // KVH, HD)
    scores = jnp.einsum("rkgd,rtkd->rkgt", asked, key_part) * (HD ** -0.5)
    positions = jnp.arange(CTX, dtype=jnp.int32)
    live_mask = positions[None, None, None, :] <= last_live[:, None, None, None]
    scores = jnp.where(live_mask, scores, -1e30)
    row_max = jnp.max(scores, axis=-1, keepdims=True)
    exp_terms = jnp.exp(scores - row_max)
    weights = (exp_terms / jnp.sum(exp_terms, axis=-1, keepdims=True)).astype(jnp.bfloat16)
    mixed_out = jnp.einsum("rkgt,rtkd->rkgd", weights.astype(jnp.float32), value_part)
    return mixed_out.reshape(REQ, QH * HD).astype(jnp.bfloat16)


def reference(x_first, x_second, w_kv, q_first, q_second, kv_cache, page_table, lengths, mig_req):
    def one_instance(inputs):
        hidden_first, hidden_second, asked_first, asked_second, pool_pages, page_rows, length, chosen = inputs
        kv_first = jnp.dot(hidden_first, w_kv, preferred_element_type=jnp.float32).astype(jnp.bfloat16)
        kv_second = jnp.dot(hidden_second, w_kv, preferred_element_type=jnp.float32).astype(jnp.bfloat16)
        gathered = pool_pages[page_rows].reshape(REQ, CTX, 2 * KVH * HD)
        first_rows = insert_rows(gathered, kv_first, length)
        second_rows = insert_rows(first_rows, kv_second, length + 1)
        out_first = softmax_read(asked_first, first_rows, length)
        out_second = softmax_read(asked_second, second_rows, length + 1)
        moving = second_rows[chosen]
        moving_len = length[chosen]
        positions = jnp.arange(CTX, dtype=jnp.int32)
        keep_mask = positions[None, :] <= moving_len[:, None] + 1
        moving = jnp.where(keep_mask[:, :, None], moving, jnp.zeros_like(moving))
        return out_first, out_second, moving

    inputs = (
        x_first.reshape(N_INST, REQ, D),
        x_second.reshape(N_INST, REQ, D),
        q_first.reshape(N_INST, REQ, QH * HD),
        q_second.reshape(N_INST, REQ, QH * HD),
        kv_cache.reshape(N_INST, POOL, PAGE, 2 * KVH * HD),
        page_table.reshape(N_INST, REQ, MAXP),
        lengths.reshape(N_INST, REQ),
        mig_req,
    )
    out_first, out_second, moving = lax.map(one_instance, inputs)
    moving = jnp.roll(moving, N_INST // 2, axis=0)
    return (out_first.reshape(NREQ, QH * HD),
            out_second.reshape(NREQ, QH * HD),
            moving.reshape(NMIG, CTX, 2 * KVH * HD))
```

```python
import functools

import jax
import jax.numpy as jnp
from jax import lax
from jax.experimental import pallas as pl
from jax.experimental.pallas import tpu as pltpu
from jax.sharding import PartitionSpec as P

HD = 128
HEADS = 8
PAGE = 16
REQ = 16
MAXP = 32
MIG = 8
CTX = 512
WIDE = 2 * HD
SLOTS = MIG * MAXP
FIRST = 64
SIZES = (80, 96, 112, 128, 144, 160, 176, 192, 208, 224, 240, 256)
SMEM = pl.BlockSpec(memory_space=pltpu.SMEM)
VMEM = pl.BlockSpec(memory_space=pltpu.VMEM)
ANY = pl.BlockSpec(memory_space=pltpu.HBM)


def requests_of(inst, mig_ref, len_ref):
    found = []
    offset = jnp.int32(MIG)
    for m in range(MIG):
        row = mig_ref[m, inst]
        length = len_ref[inst * REQ + row]
        whole = length // PAGE
        found.append((row, length, whole, offset))
        offset = offset + whole
    return found, offset


def wait_pages(ref, sem, count):
    for bit in range(9):
        size = 1 << bit
        if size <= ref.shape[0]:

            @pl.when((count >> bit) & 1 == 1)
            def _(size=size):
                part = ref.at[pl.ds(0, size)]
                pltpu.make_async_copy(part, part, sem).wait()


def pack_whole(found, table_ref, pool_ref, out_ref, sem, low, high, base):
    count = jnp.int32(0)
    for row, _, whole, offset in found:
        start = jnp.clip(low - offset, 0, whole)
        stop = jnp.clip(high - offset, 0, whole)

        def body(p, _, row=row, offset=offset):
            pltpu.make_async_copy(
                pool_ref.at[table_ref[row, p]], out_ref.at[offset + p - base], sem
            ).start()
            return 0

        lax.fori_loop(start, stop, body, 0)
        count = count + stop - start
    return count


def pack_first_kernel(table_ref, len_ref, mig_ref, pool_ref, out_ref, size_ref, sem):
    inst = lax.axis_index("inst")
    half = lax.axis_size("inst") // 2
    found, total = requests_of(inst, mig_ref, len_ref)
    for m, (row, _, whole, _) in enumerate(found):
        pltpu.make_async_copy(pool_ref.at[table_ref[row, whole]], out_ref.at[m], sem).start()
    count = MIG + pack_whole(found, table_ref, pool_ref, out_ref, sem, MIG, FIRST, 0)
    partner = lax.rem(inst + half, 2 * half)
    _, other = requests_of(partner, mig_ref, len_ref)
    most = jnp.maximum(total, other)
    choice = jnp.int32(0)
    for size in SIZES[:-1]:
        choice = choice + jnp.where(most > size, 1, 0)
    size_ref[0] = choice
    wait_pages(out_ref, sem, count)


def pack_rest_kernel(size, table_ref, len_ref, mig_ref, pool_ref, out_ref, sem):
    inst = lax.axis_index("inst")
    found, _ = requests_of(inst, mig_ref, len_ref)
    count = pack_whole(found, table_ref, pool_ref, out_ref, sem, FIRST, size, FIRST)
    wait_pages(out_ref, sem, count)


def copy_run(src_ref, src, dst_ref, dst, count, most, sem):
    for bit in range(most.bit_length() - 1, -1, -1):
        size = 1 << bit
        taken = (count >> (bit + 1)) << (bit + 1)

        @pl.when((count >> bit) & 1 == 1)
        def _(size=size, taken=taken):
            pltpu.make_async_copy(
                src_ref.at[pl.ds(src + taken, size)], dst_ref.at[pl.ds(dst + taken, size)], sem
            ).start()


def unpack_whole(found, got_ref, out_ref, sem, low, high, base):
    count = jnp.int32(0)
    for m, (_, _, whole, offset) in enumerate(found):
        start = jnp.clip(low - offset, 0, whole)
        stop = jnp.clip(high - offset, 0, whole)
        copy_run(got_ref, offset + start - base, out_ref, m * MAXP + start, stop - start, 31, sem)
        count = count + stop - start
    return count


def unpack_first_kernel(len_ref, mig_ref, got_ref, fresh_ref, out_ref, zeros, rows, made, sem):
    inst = lax.axis_index("inst")
    half = lax.axis_size("inst") // 2
    partner = lax.rem(inst + half, 2 * half)
    found, _ = requests_of(partner, mig_ref, len_ref)
    zeros[...] = jnp.zeros_like(zeros)
    rows[...] = fresh_ref[...].astype(jnp.float32)
    count = unpack_whole(found, got_ref, out_ref, sem, MIG, FIRST, 0)
    for m, (_, _, whole, _) in enumerate(found):
        empty = jnp.maximum(MAXP - 2 - whole, 0)
        copy_run(zeros, 0, out_ref, m * MAXP + whole + 2, empty, MAXP - 2, sem)
        count = count + empty
    place = lax.broadcasted_iota(jnp.int32, (PAGE, WIDE), 0)
    for m, (row, length, whole, _) in enumerate(found):
        rest = lax.rem(length, PAGE)
        first = rows[pl.ds(row, 1), :]
        second = rows[pl.ds(REQ + row, 1), :]
        page = jnp.where(place < rest, got_ref[m].astype(jnp.float32), 0.0)
        page = jnp.where(place == rest, first, page)
        page = jnp.where(place == rest + 1, second, page)
        made[m, 0] = page.astype(jnp.bfloat16)
        made[m, 1] = jnp.where(place == rest + 1 - PAGE, second, 0.0).astype(jnp.bfloat16)
        both = whole + 1 < MAXP

        @pl.when(both)
        def _(m=m, whole=whole):
            pltpu.make_async_copy(made.at[m], out_ref.at[pl.ds(m * MAXP + whole, 2)], sem).start()

        @pl.when(jnp.logical_not(both))
        def _(m=m, whole=whole):
            pltpu.make_async_copy(
                made.at[m, pl.ds(0, 1)], out_ref.at[pl.ds(m * MAXP + whole, 1)], sem
            ).start()

        count = count + jnp.where(both, 2, 1)
    wait_pages(out_ref, sem, count)


def unpack_rest_kernel(size, len_ref, mig_ref, got_ref, old_ref, out_ref, sem):
    inst = lax.axis_index("inst")
    half = lax.axis_size("inst") // 2
    partner = lax.rem(inst + half, 2 * half)
    found, _ = requests_of(partner, mig_ref, len_ref)
    count = unpack_whole(found, got_ref, out_ref, sem, FIRST, size, FIRST)
    wait_pages(out_ref, sem, count)


def attend_kernel(table_ref, len_ref, query_ref, fresh_ref, pool_ref, out_ref, tokens):
    inst = lax.axis_index("inst")
    place = lax.broadcasted_iota(jnp.int32, (PAGE, WIDE), 0)
    position = lax.broadcasted_iota(jnp.int32, (2 * HEADS, CTX), 1)
    late = jnp.where(lax.broadcasted_iota(jnp.int32, (2 * HEADS, CTX), 0) >= HEADS, 1, 0)

    def pair(step, _):
        for lane in range(2):
            r = step * 2 + lane
            length = len_ref[inst * REQ + r]
            whole = length // PAGE
            rest = lax.rem(length, PAGE)
            for p in range(MAXP):
                tokens[lane, pl.ds(p * PAGE, PAGE), :] = pool_ref[table_ref[r, p]]
            first = fresh_ref[pl.ds(r, 1), :]
            second = fresh_ref[pl.ds(REQ + r, 1), :]
            at = pl.ds(pl.multiple_of(whole * PAGE, PAGE), PAGE)
            page = tokens[lane, at, :].astype(jnp.float32)
            page = jnp.where(place == rest, first, page)
            page = jnp.where(place == rest + 1, second, page)
            tokens[lane, at, :] = page.astype(jnp.bfloat16)
            at = pl.ds(pl.multiple_of(jnp.minimum(whole + 1, MAXP - 1) * PAGE, PAGE), PAGE)
            page = tokens[lane, at, :].astype(jnp.float32)
            page = jnp.where(place == rest + 1 - PAGE, second, page)
            tokens[lane, at, :] = page.astype(jnp.bfloat16)
            scores = lax.dot_general(
                query_ref[r],
                tokens[lane, :, :HD],
                (((1,), (1,)), ((), ())),
                preferred_element_type=jnp.float32,
            ) * HD ** (-0.5)
            scores = jnp.where(position <= length + late, scores, -1e30)
            terms = jnp.exp(scores - jnp.max(scores, axis=-1, keepdims=True))
            weights = (terms / jnp.sum(terms, axis=-1, keepdims=True)).astype(jnp.bfloat16)
            mixed = jnp.dot(weights, tokens[lane, :, HD:], preferred_element_type=jnp.float32)
            out_ref[r] = mixed.astype(jnp.bfloat16)
        return 0

    lax.fori_loop(0, REQ // 2, pair, 0)


def page_array(count):
    return jax.ShapeDtypeStruct((count, PAGE, WIDE), jnp.bfloat16)


def attend(page_table, lengths, queries, fresh, kv_cache):
    return pl.pallas_call(
        attend_kernel,
        out_shape=jax.ShapeDtypeStruct((REQ, 2 * HEADS, HD), jnp.bfloat16),
        in_specs=[SMEM, SMEM, VMEM, VMEM, VMEM],
        out_specs=VMEM,
        scratch_shapes=[pltpu.VMEM((2, CTX, WIDE), jnp.bfloat16)],
        compiler_params=pltpu.CompilerParams(vmem_limit_bytes=24 << 20),
        cost_estimate=pl.CostEstimate(flops=70_000_000, bytes_accessed=40 << 20, transcendentals=130_000),
        name="attend",
    )(page_table, lengths, queries, fresh, kv_cache)


def swap(block):
    count = lax.axis_size("inst")
    return lax.ppermute(block, "inst", [(i, (i + count // 2) % count) for i in range(count)])


def local(x_first, x_second, w_kv, q_first, q_second, kv_cache, page_table, lengths, mig_req):
    moving = mig_req.T
    packed, choice = pl.pallas_call(
        pack_first_kernel,
        out_shape=(page_array(FIRST), jax.ShapeDtypeStruct((1,), jnp.int32)),
        in_specs=[SMEM, SMEM, SMEM, ANY],
        out_specs=(VMEM, SMEM),
        scratch_shapes=[pltpu.SemaphoreType.DMA],
        name="pack_first",
    )(page_table, lengths, moving, kv_cache)

    def branch(size, packed, x_first, x_second, w_kv, q_first, q_second, kv_cache, page_table, lengths, moving):
        got_first = swap(packed)
        rest = pl.pallas_call(
            functools.partial(pack_rest_kernel, size),
            out_shape=page_array(size - FIRST),
            in_specs=[SMEM, SMEM, SMEM, ANY],
            out_specs=VMEM,
            scratch_shapes=[pltpu.SemaphoreType.DMA],
            name="pack_rest",
        )(page_table, lengths, moving, kv_cache)
        got_rest = swap(rest)
        hidden = jnp.concatenate([x_first, x_second], 0)
        share = jnp.dot(hidden, w_kv, preferred_element_type=jnp.float32)
        shares = lax.all_to_all(share.reshape(2 * REQ, 4, WIDE), "tp", split_axis=1, concat_axis=0, tiled=False)
        fresh = jnp.sum(shares, axis=0)
        got_fresh = swap(fresh.astype(jnp.bfloat16))
        queries = jnp.stack(
            [q_first.reshape(REQ, HEADS, HD), q_second.reshape(REQ, HEADS, HD)], axis=1
        ).reshape(REQ, 2 * HEADS, HD)
        mixed = attend(page_table, lengths, queries, fresh, kv_cache)
        attn_first = mixed[:, :HEADS].reshape(REQ, HEADS * HD)
        attn_second = mixed[:, HEADS:].reshape(REQ, HEADS * HD)
        imported = pl.pallas_call(
            unpack_first_kernel,
            out_shape=page_array(SLOTS),
            in_specs=[SMEM, SMEM, VMEM, VMEM],
            out_specs=ANY,
            scratch_shapes=[
                pltpu.VMEM((MAXP, PAGE, WIDE), jnp.bfloat16),
                pltpu.VMEM((2 * REQ, WIDE), jnp.float32),
                pltpu.VMEM((MIG, 2, PAGE, WIDE), jnp.bfloat16),
                pltpu.SemaphoreType.DMA,
            ],
            name="unpack_first",
        )(lengths, moving, got_first, got_fresh)
        imported = pl.pallas_call(
            functools.partial(unpack_rest_kernel, size),
            out_shape=page_array(SLOTS),
            in_specs=[SMEM, SMEM, VMEM, ANY],
            out_specs=ANY,
            scratch_shapes=[pltpu.SemaphoreType.DMA],
            input_output_aliases={3: 0},
            name="unpack_rest",
        )(lengths, moving, got_rest, imported)
        return attn_first, attn_second, imported.reshape(MIG, CTX, WIDE)

    return lax.switch(
        choice[0],
        [functools.partial(branch, size) for size in SIZES],
        packed, x_first, x_second, w_kv, q_first, q_second, kv_cache, page_table, lengths, moving,
    )


def solution(mesh):
    return jax.shard_map(
        local,
        mesh=mesh,
        in_specs=(
            P("inst", "tp"),
            P("inst", "tp"),
            P("tp", None),
            P("inst", "tp"),
            P("inst", "tp"),
            P("inst", None, "tp"),
            P("inst", None),
            P(),
            P(),
        ),
        out_specs=(P("inst", "tp"), P("inst", "tp"), P("inst", None, "tp")),
        check_vma=False,
    )
```

```python
import functools

import jax
import jax.numpy as jnp
from jax import lax
from jax.experimental import pallas as pl
from jax.experimental.pallas import tpu as pltpu
from jax.sharding import PartitionSpec as P

HD = 128
HEADS = 8
PAGE = 16
REQ = 16
MAXP = 32
MIG = 8
CTX = 512
WIDE = 2 * HD
SLOTS = MIG * MAXP
FIRST = 112
REST = SLOTS - FIRST
SIZES = tuple(range(8, REST + 1, 8))
SMEM = pl.BlockSpec(memory_space=pltpu.SMEM)
VMEM = pl.BlockSpec(memory_space=pltpu.VMEM)
ANY = pl.BlockSpec(memory_space=pltpu.HBM)


def requests_of(inst, mig_ref, len_ref):
    found = []
    offset = jnp.int32(MIG)
    for m in range(MIG):
        row = mig_ref[m, inst]
        length = len_ref[inst * REQ + row]
        whole = lax.shift_right_logical(length, 4)
        found.append((row, length, whole, offset))
        offset = offset + whole
    return found, offset


def wait_pages(ref, sem, count):
    for bit in range(9):
        size = 1 << bit
        if size <= ref.shape[0]:

            @pl.when((count >> bit) & 1 == 1)
            def _(size=size):
                part = ref.at[pl.ds(0, size)]
                pltpu.make_async_copy(part, part, sem).wait()


def pack_whole(found, table_ref, pool_ref, out_ref, sem, low, high, base):
    count = jnp.int32(0)
    for row, _, whole, offset in found:
        start = jnp.clip(low - offset, 0, whole)
        stop = jnp.clip(high - offset, 0, whole)

        def body(p, _, row=row, offset=offset):
            pltpu.make_async_copy(
                pool_ref.at[table_ref[row, p]], out_ref.at[offset + p - base], sem
            ).start()
            return 0

        lax.fori_loop(start, stop, body, 0)
        count = count + stop - start
    return count


def pack_first_kernel(table_ref, len_ref, mig_ref, pool_ref, out_ref, sem):
    inst = lax.axis_index("inst")
    found, _ = requests_of(inst, mig_ref, len_ref)
    for m, (row, _, whole, _) in enumerate(found):
        pltpu.make_async_copy(pool_ref.at[table_ref[row, whole]], out_ref.at[m], sem).start()
    count = MIG + pack_whole(found, table_ref, pool_ref, out_ref, sem, MIG, FIRST, 0)
    wait_pages(out_ref, sem, count)


def pack_rest_kernel(table_ref, len_ref, mig_ref, pool_ref, out_ref, size_ref, sem):
    inst = lax.axis_index("inst")
    half = lax.axis_size("inst") // 2
    found, total = requests_of(inst, mig_ref, len_ref)
    count = pack_whole(found, table_ref, pool_ref, out_ref, sem, FIRST, SLOTS, FIRST)
    partner = lax.rem(inst + half, 2 * half)
    _, other = requests_of(partner, mig_ref, len_ref)
    most = jnp.maximum(total, other) - FIRST
    choice = jnp.int32(0)
    for size in SIZES[:-1]:
        choice = choice + jnp.where(most > size, 1, 0)
    size_ref[0] = choice
    wait_pages(out_ref, sem, count)


def copy_run(src_ref, src, dst_ref, dst, count, most, sem):
    for bit in range(most.bit_length() - 1, -1, -1):
        size = 1 << bit
        taken = (count >> (bit + 1)) << (bit + 1)

        @pl.when((count >> bit) & 1 == 1)
        def _(size=size, taken=taken):
            pltpu.make_async_copy(
                src_ref.at[pl.ds(src + taken, size)], dst_ref.at[pl.ds(dst + taken, size)], sem
            ).start()


def unpack_whole(found, got_ref, out_ref, sem, low, high, base):
    count = jnp.int32(0)
    for m, (_, _, whole, offset) in enumerate(found):
        start = jnp.clip(low - offset, 0, whole)
        stop = jnp.clip(high - offset, 0, whole)
        copy_run(got_ref, offset + start - base, out_ref, m * MAXP + start, stop - start, 31, sem)
        count = count + stop - start
    return count


def partner_requests(mig_ref, len_ref):
    half = lax.axis_size("inst") // 2
    partner = lax.rem(lax.axis_index("inst") + half, 2 * half)
    return requests_of(partner, mig_ref, len_ref)[0]


def clear_kernel(len_ref, mig_ref, out_ref, zeros, sem):
    found = partner_requests(mig_ref, len_ref)
    zeros[...] = jnp.zeros_like(zeros)
    count = jnp.int32(0)
    for m, (_, _, whole, _) in enumerate(found):
        empty = jnp.maximum(MAXP - 2 - whole, 0)
        copy_run(zeros, 0, out_ref, m * MAXP + whole + 2, empty, MAXP - 2, sem)
        count = count + empty
    wait_pages(out_ref, sem, count)


def unpack_kernel(len_ref, mig_ref, first_ref, rest_ref, fresh_ref, old_ref, out_ref, rows, made, sem):
    found = partner_requests(mig_ref, len_ref)
    count = unpack_whole(found, first_ref, out_ref, sem, MIG, FIRST, 0)
    count = count + unpack_whole(found, rest_ref, out_ref, sem, FIRST, SLOTS, FIRST)
    rows[...] = fresh_ref[...].astype(jnp.float32)
    place = lax.broadcasted_iota(jnp.int32, (PAGE, WIDE), 0)
    for m, (row, length, whole, _) in enumerate(found):
        rest = length & (PAGE - 1)
        first = rows[pl.ds(row, 1), :]
        second = rows[pl.ds(REQ + row, 1), :]
        page = jnp.where(place < rest, first_ref[m].astype(jnp.float32), 0.0)
        page = jnp.where(place == rest, first, page)
        page = jnp.where(place == rest + 1, second, page)
        made[m, 0] = page.astype(jnp.bfloat16)
        made[m, 1] = jnp.where(place == rest + 1 - PAGE, second, 0.0).astype(jnp.bfloat16)
        both = whole + 1 < MAXP

        @pl.when(both)
        def _(m=m, whole=whole):
            pltpu.make_async_copy(made.at[m], out_ref.at[pl.ds(m * MAXP + whole, 2)], sem).start()

        @pl.when(jnp.logical_not(both))
        def _(m=m, whole=whole):
            pltpu.make_async_copy(
                made.at[m, pl.ds(0, 1)], out_ref.at[pl.ds(m * MAXP + whole, 1)], sem
            ).start()

        count = count + jnp.where(both, 2, 1)
    wait_pages(out_ref, sem, count)


def attend_kernel(table_ref, len_ref, query_ref, fresh_ref, pool_ref, out_ref, tokens):
    inst = lax.axis_index("inst")
    place = lax.broadcasted_iota(jnp.int32, (PAGE, WIDE), 0)
    position = lax.broadcasted_iota(jnp.int32, (2 * HEADS, CTX), 1)
    late = jnp.where(lax.broadcasted_iota(jnp.int32, (2 * HEADS, CTX), 0) >= HEADS, 1, 0)

    def pair(step, _):
        for lane in range(2):
            r = step * 2 + lane
            length = len_ref[inst * REQ + r]
            whole = lax.shift_right_logical(length, 4)
            rest = length & (PAGE - 1)
            for p in range(MAXP):
                tokens[lane, pl.ds(p * PAGE, PAGE), :] = pool_ref[table_ref[r, p]]
            first = fresh_ref[pl.ds(r, 1), :]
            second = fresh_ref[pl.ds(REQ + r, 1), :]
            at = pl.ds(pl.multiple_of(whole * PAGE, PAGE), PAGE)
            page = tokens[lane, at, :].astype(jnp.float32)
            page = jnp.where(place == rest, first, page)
            page = jnp.where(place == rest + 1, second, page)
            tokens[lane, at, :] = page.astype(jnp.bfloat16)
            at = pl.ds(pl.multiple_of(jnp.minimum(whole + 1, MAXP - 1) * PAGE, PAGE), PAGE)
            page = tokens[lane, at, :].astype(jnp.float32)
            page = jnp.where(place == rest + 1 - PAGE, second, page)
            tokens[lane, at, :] = page.astype(jnp.bfloat16)
            scores = lax.dot_general(
                query_ref[r],
                tokens[lane, :, :HD],
                (((1,), (1,)), ((), ())),
                preferred_element_type=jnp.float32,
            ) * HD ** (-0.5)
            scores = jnp.where(position <= length + late, scores, -1e30)
            terms = jnp.exp(scores - jnp.max(scores, axis=-1, keepdims=True))
            weights = (terms / jnp.sum(terms, axis=-1, keepdims=True)).astype(jnp.bfloat16)
            mixed = jnp.dot(weights, tokens[lane, :, HD:], preferred_element_type=jnp.float32)
            out_ref[r] = mixed.astype(jnp.bfloat16)
        return 0

    lax.fori_loop(0, REQ // 2, pair, 0)


def page_array(count):
    return jax.ShapeDtypeStruct((count, PAGE, WIDE), jnp.bfloat16)


def attend(page_table, lengths, queries, fresh, kv_cache):
    return pl.pallas_call(
        attend_kernel,
        out_shape=jax.ShapeDtypeStruct((REQ, 2 * HEADS, HD), jnp.bfloat16),
        in_specs=[SMEM, SMEM, VMEM, VMEM, VMEM],
        out_specs=VMEM,
        scratch_shapes=[pltpu.VMEM((2, CTX, WIDE), jnp.bfloat16)],
        compiler_params=pltpu.CompilerParams(vmem_limit_bytes=24 << 20),
        cost_estimate=pl.CostEstimate(flops=70_000_000, bytes_accessed=40 << 20, transcendentals=130_000),
        name="attend",
    )(page_table, lengths, queries, fresh, kv_cache)


def swap(block):
    count = lax.axis_size("inst")
    return lax.ppermute(block, "inst", [(i, (i + count // 2) % count) for i in range(count)])


def local(x_first, x_second, w_kv, q_first, q_second, kv_cache, page_table, lengths, mig_req):
    moving = mig_req.T
    first = pl.pallas_call(
        pack_first_kernel,
        out_shape=pltpu.VMEM((FIRST, PAGE, WIDE), jnp.bfloat16),
        in_specs=[SMEM, SMEM, SMEM, ANY],
        out_specs=VMEM,
        scratch_shapes=[pltpu.SemaphoreType.DMA],
        name="pack_first",
    )(page_table, lengths, moving, kv_cache)
    got_first = swap(first)
    rest, choice = pl.pallas_call(
        pack_rest_kernel,
        out_shape=(pltpu.VMEM((REST, PAGE, WIDE), jnp.bfloat16), jax.ShapeDtypeStruct((1,), jnp.int32)),
        in_specs=[SMEM, SMEM, SMEM, ANY],
        out_specs=(VMEM, SMEM),
        scratch_shapes=[pltpu.SemaphoreType.DMA],
        name="pack_rest",
    )(page_table, lengths, moving, kv_cache)
    blank = pl.pallas_call(
        clear_kernel,
        out_shape=page_array(SLOTS),
        in_specs=[SMEM, SMEM],
        out_specs=ANY,
        scratch_shapes=[pltpu.VMEM((MAXP, PAGE, WIDE), jnp.bfloat16), pltpu.SemaphoreType.DMA],
        name="clear",
    )(lengths, moving)
    hidden = jnp.concatenate([x_first, x_second], 0)
    share = jnp.dot(hidden, w_kv, preferred_element_type=jnp.float32)
    shares = lax.all_to_all(share.reshape(2 * REQ, 4, WIDE), "tp", split_axis=1, concat_axis=0, tiled=False)
    fresh = jnp.sum(shares, axis=0)
    got_fresh = swap(fresh.astype(jnp.bfloat16))
    queries = jnp.stack(
        [q_first.reshape(REQ, HEADS, HD), q_second.reshape(REQ, HEADS, HD)], axis=1
    ).reshape(REQ, 2 * HEADS, HD)
    mixed = attend(page_table, lengths, queries, fresh, kv_cache)
    attn_first = mixed[:, :HEADS].reshape(REQ, HEADS * HD)
    attn_second = mixed[:, HEADS:].reshape(REQ, HEADS * HD)
    choice, rest, attn_first, attn_second, blank = lax.optimization_barrier(
        (choice, rest, attn_first, attn_second, blank)
    )

    def branch(size, rest):
        return lax.pad(swap(rest[:size]), jnp.zeros((), jnp.bfloat16), ((0, REST - size, 0), (0, 0, 0), (0, 0, 0)))

    got_rest = lax.switch(choice[0], [functools.partial(branch, size) for size in SIZES], rest)
    got_first, got_rest, got_fresh = (
        pltpu.with_memory_space_constraint(got, pltpu.VMEM) for got in (got_first, got_rest, got_fresh)
    )
    imported = pl.pallas_call(
        unpack_kernel,
        out_shape=page_array(SLOTS),
        in_specs=[SMEM, SMEM, VMEM, VMEM, VMEM, ANY],
        out_specs=ANY,
        scratch_shapes=[
            pltpu.VMEM((2 * REQ, WIDE), jnp.float32),
            pltpu.VMEM((MIG, 2, PAGE, WIDE), jnp.bfloat16),
            pltpu.SemaphoreType.DMA,
        ],
        input_output_aliases={5: 0},
        name="unpack",
    )(lengths, moving, got_first, got_rest, got_fresh, blank)
    return attn_first, attn_second, imported.reshape(MIG, CTX, WIDE)


def solution(mesh):
    return jax.shard_map(
        local,
        mesh=mesh,
        in_specs=(
            P("inst", "tp"),
            P("inst", "tp"),
            P("tp", None),
            P("inst", "tp"),
            P("inst", "tp"),
            P("inst", None, "tp"),
            P("inst", None),
            P(),
            P(),
        ),
        out_specs=(P("inst", "tp"), P("inst", "tp"), P("inst", None, "tp")),
        check_vma=False,
    )
```

```python
import functools

import jax
import jax.numpy as jnp
from jax import lax
from jax.experimental import pallas as pl
from jax.experimental.pallas import tpu as pltpu
from jax.sharding import PartitionSpec as P

HD = 128
HEADS = 8
PAGE = 16
REQ = 16
MAXP = 32
MIG = 8
CTX = 512
WIDE = 2 * HD
SLOTS = MIG * MAXP
GROUP = 2
FIRST = 112
MOVED = 24
FIXED = FIRST + MOVED
HEAD = 2 * REQ // PAGE
REST = SLOTS - FIXED
SIZES = (16, 24, 32, 40, 48, 56, 72, REST)
LIGHT = pl.CostEstimate(flops=1, bytes_accessed=1, transcendentals=0)
SMEM = pl.BlockSpec(memory_space=pltpu.SMEM)
VMEM = pl.BlockSpec(memory_space=pltpu.VMEM)
ANY = pl.BlockSpec(memory_space=pltpu.HBM)


def requests_of(inst, mig_ref, len_ref):
    found = []
    offset = jnp.int32(MIG)
    for m in range(MIG):
        row = mig_ref[m, inst]
        length = len_ref[inst * REQ + row]
        whole = lax.shift_right_logical(length, 4)
        found.append((row, length, whole, offset))
        offset = offset + whole
    return found, offset


def wait_pages(ref, sem, count):
    for bit in range(9):
        size = 1 << bit
        if size <= ref.shape[0]:

            @pl.when((count >> bit) & 1 == 1)
            def _(size=size):
                part = ref.at[pl.ds(0, size)]
                pltpu.make_async_copy(part, part, sem).wait()


def pack_whole(found, table_ref, pool_ref, out_ref, sem, low, high, base):
    count = jnp.int32(0)
    for row, _, whole, offset in found:
        start = jnp.clip(low - offset, 0, whole)
        stop = jnp.clip(high - offset, 0, whole)

        def body(p, _, row=row, offset=offset):
            pltpu.make_async_copy(
                pool_ref.at[table_ref[row, p]], out_ref.at[offset + p - base], sem
            ).start()
            return 0

        lax.fori_loop(start, stop, body, 0)
        count = count + stop - start
    return count


def pack_first_kernel(table_ref, len_ref, mig_ref, pool_ref, out_ref, sem):
    inst = lax.axis_index("inst")
    found, _ = requests_of(inst, mig_ref, len_ref)
    for m, (row, _, whole, _) in enumerate(found):
        pltpu.make_async_copy(pool_ref.at[table_ref[row, whole]], out_ref.at[m], sem).start()
    count = MIG + pack_whole(found, table_ref, pool_ref, out_ref, sem, MIG, FIRST, 0)
    wait_pages(out_ref, sem, count)


def pages_of(inst, mig_ref, len_ref):
    total = jnp.int32(MIG)
    for m in range(MIG):
        total = total + lax.shift_right_logical(len_ref[inst * REQ + mig_ref[m, inst]], 4)
    return total


def plan_kernel(table_ref, len_ref, mig_ref, pool_ref, out_ref, plan_ref, sem):
    inst = lax.axis_index("inst")
    half = lax.axis_size("inst") // 2
    partner = lax.rem(inst + half, 2 * half)
    rows = []
    for one in (inst, partner):
        base = one & ~(2 * (GROUP - 1))
        rows.append([pages_of(base + 2 * j, mig_ref, len_ref) for j in range(GROUP)])

    def short(limit):
        bad = jnp.bool_(False)
        for totals in rows:
            spare = jnp.int32(0)
            for total in totals:
                over = total - limit
                spare = spare - jnp.maximum(over, -MOVED)
                bad = jnp.logical_or(bad, over > MOVED)
            bad = jnp.logical_or(bad, spare < 0)
        return bad

    choice = jnp.int32(0)
    limit = jnp.int32(FIXED + SIZES[0])
    for n in range(1, len(SIZES)):
        worse = short(limit)
        choice = jnp.where(worse, n, choice)
        limit = jnp.where(worse, FIXED + SIZES[n], limit)
    plan_ref[0] = choice
    plan_ref[1] = limit
    for side, totals in enumerate(rows):
        at = 2 + side * 4 * GROUP
        begin = jnp.int32(0)
        for j, total in enumerate(totals):
            given = jnp.maximum(total - limit, 0)
            plan_ref[at + j] = begin
            plan_ref[at + GROUP + j] = given
            begin = begin + given
        every = begin
        begin = jnp.int32(0)
        for j, total in enumerate(totals):
            room = jnp.clip(limit - total, 0, MOVED)
            taken = jnp.clip(every - begin, 0, room)
            plan_ref[at + 2 * GROUP + j] = begin
            plan_ref[at + 3 * GROUP + j] = taken
            begin = begin + taken
    found, _ = requests_of(inst, mig_ref, len_ref)
    count = pack_whole(found, table_ref, pool_ref, out_ref, sem, limit, SLOTS, limit)
    wait_pages(out_ref, sem, count)


def windows(taken, limit):
    last = FIRST - taken + MOVED
    return (FIRST, last, FIRST - taken - HEAD), (last, limit, last)


def pack_rest_kernel(
    table_ref, len_ref, mig_ref, plan_ref, given_ref, fresh_ref, pool_ref, second_ref, last_ref, sems
):
    inst = lax.axis_index("inst")
    member = lax.shift_right_logical(inst, 1) & (GROUP - 1)
    found, _ = requests_of(inst, mig_ref, len_ref)
    begin = plan_ref[2 + 2 * GROUP + member]
    taken = plan_ref[2 + 3 * GROUP + member]
    parts = windows(taken, plan_ref[1])
    counts = []
    for n, (out_ref, (low, high, base)) in enumerate(zip((second_ref, last_ref), parts)):
        counts.append(pack_whole(found, table_ref, pool_ref, out_ref, sems.at[n], low, high, base))

    @pl.when(taken > 0)
    def _():
        for j in range(GROUP):
            start = jnp.maximum(plan_ref[2 + j], begin)
            stop = jnp.minimum(plan_ref[2 + j] + plan_ref[2 + GROUP + j], begin + taken)
            copy_run(
                given_ref,
                start - plan_ref[2 + j],
                second_ref,
                HEAD + start - begin,
                jnp.maximum(stop - start, 0),
                MOVED,
                sems.at[0],
            )

    counts[0] = counts[0] + taken
    second_ref[pl.ds(0, HEAD)] = fresh_ref[...].reshape(HEAD, PAGE, WIDE).astype(jnp.bfloat16)
    for n, out_ref in enumerate((second_ref, last_ref)):
        wait_pages(out_ref, sems.at[n], counts[n])


def copy_run(src_ref, src, dst_ref, dst, count, most, sem):
    for bit in range(most.bit_length() - 1, -1, -1):
        size = 1 << bit
        taken = (count >> (bit + 1)) << (bit + 1)

        @pl.when((count >> bit) & 1 == 1)
        def _(size=size, taken=taken):
            pltpu.make_async_copy(
                src_ref.at[pl.ds(src + taken, size)], dst_ref.at[pl.ds(dst + taken, size)], sem
            ).start()


def unpack_whole(found, got_ref, out_ref, sem, low, high, base):
    count = jnp.int32(0)
    for m, (_, _, whole, offset) in enumerate(found):
        start = jnp.clip(low - offset, 0, whole)
        stop = jnp.clip(high - offset, 0, whole)
        copy_run(got_ref, offset + start - base, out_ref, m * MAXP + start, stop - start, 31, sem)
        count = count + stop - start
    return count


def partner_requests(mig_ref, len_ref):
    half = lax.axis_size("inst") // 2
    partner = lax.rem(lax.axis_index("inst") + half, 2 * half)
    return requests_of(partner, mig_ref, len_ref)[0]


def clear_kernel(len_ref, mig_ref, out_ref, zeros, sem):
    found = partner_requests(mig_ref, len_ref)
    zeros[...] = jnp.zeros_like(zeros)
    count = jnp.int32(0)
    for m, (_, _, whole, _) in enumerate(found):
        empty = jnp.maximum(MAXP - 2 - whole, 0)
        copy_run(zeros, 0, out_ref, m * MAXP + whole + 2, empty, MAXP - 2, sem)
        count = count + empty
    wait_pages(out_ref, sem, count)


def unpack_kernel(
    len_ref, mig_ref, plan_ref, first_ref, second_ref, last_ref, back_ref, old_ref, out_ref, rows, made, sem
):
    member = lax.shift_right_logical(lax.axis_index("inst"), 1) & (GROUP - 1)
    found = partner_requests(mig_ref, len_ref)
    limit = plan_ref[1]
    at = 2 + 4 * GROUP
    taken = plan_ref[at + 3 * GROUP + member]
    count = unpack_whole(found, first_ref, out_ref, sem, MIG, FIRST, 0)
    for got_ref, (low, high, base) in zip((second_ref, last_ref), windows(taken, limit)):
        count = count + unpack_whole(found, got_ref, out_ref, sem, low, high, base)
    begin = plan_ref[at + member]
    given = plan_ref[at + GROUP + member]

    @pl.when(given > 0)
    def _():
        for j in range(GROUP):
            base = limit + plan_ref[at + 2 * GROUP + j] - begin
            low = jnp.maximum(base, limit)
            high = jnp.maximum(base + plan_ref[at + 3 * GROUP + j], low)
            unpack_whole(found, back_ref, out_ref, sem, low, high, base)

    count = count + given
    rows[...] = second_ref[pl.ds(0, HEAD)].astype(jnp.float32).reshape(2 * REQ, WIDE)
    place = lax.broadcasted_iota(jnp.int32, (PAGE, WIDE), 0)
    for m, (row, length, whole, _) in enumerate(found):
        rest = length & (PAGE - 1)
        first = rows[pl.ds(row, 1), :]
        second = rows[pl.ds(REQ + row, 1), :]
        page = jnp.where(place < rest, first_ref[m].astype(jnp.float32), 0.0)
        page = jnp.where(place == rest, first, page)
        page = jnp.where(place == rest + 1, second, page)
        made[m, 0] = page.astype(jnp.bfloat16)
        made[m, 1] = jnp.where(place == rest + 1 - PAGE, second, 0.0).astype(jnp.bfloat16)
        both = whole + 1 < MAXP

        @pl.when(both)
        def _(m=m, whole=whole):
            pltpu.make_async_copy(made.at[m], out_ref.at[pl.ds(m * MAXP + whole, 2)], sem).start()

        @pl.when(jnp.logical_not(both))
        def _(m=m, whole=whole):
            pltpu.make_async_copy(
                made.at[m, pl.ds(0, 1)], out_ref.at[pl.ds(m * MAXP + whole, 1)], sem
            ).start()

        count = count + jnp.where(both, 2, 1)
    wait_pages(out_ref, sem, count)


def attend_kernel(table_ref, len_ref, query_ref, fresh_ref, pool_ref, out_ref, tokens):
    inst = lax.axis_index("inst")
    place = lax.broadcasted_iota(jnp.int32, (PAGE, WIDE), 0)
    position = lax.broadcasted_iota(jnp.int32, (2 * HEADS, CTX), 1)
    late = jnp.where(lax.broadcasted_iota(jnp.int32, (2 * HEADS, CTX), 0) >= HEADS, 1, 0)

    def pair(step, _):
        for lane in range(2):
            r = step * 2 + lane
            length = len_ref[inst * REQ + r]
            whole = lax.shift_right_logical(length, 4)
            rest = length & (PAGE - 1)
            for p in range(MAXP):
                tokens[lane, pl.ds(p * PAGE, PAGE), :] = pool_ref[table_ref[r, p]]
            first = fresh_ref[pl.ds(r, 1), :]
            second = fresh_ref[pl.ds(REQ + r, 1), :]
            at = pl.ds(pl.multiple_of(whole * PAGE, PAGE), PAGE)
            page = tokens[lane, at, :].astype(jnp.float32)
            page = jnp.where(place == rest, first, page)
            page = jnp.where(place == rest + 1, second, page)
            tokens[lane, at, :] = page.astype(jnp.bfloat16)
            at = pl.ds(pl.multiple_of(jnp.minimum(whole + 1, MAXP - 1) * PAGE, PAGE), PAGE)
            page = tokens[lane, at, :].astype(jnp.float32)
            page = jnp.where(place == rest + 1 - PAGE, second, page)
            tokens[lane, at, :] = page.astype(jnp.bfloat16)
            scores = lax.dot_general(
                query_ref[r],
                tokens[lane, :, :HD],
                (((1,), (1,)), ((), ())),
                preferred_element_type=jnp.float32,
            ) * HD ** (-0.5)
            scores = jnp.where(position <= length + late, scores, -1e30)
            terms = jnp.exp(scores - jnp.max(scores, axis=-1, keepdims=True))
            weights = (terms / jnp.sum(terms, axis=-1, keepdims=True)).astype(jnp.bfloat16)
            mixed = jnp.dot(weights, tokens[lane, :, HD:], preferred_element_type=jnp.float32)
            out_ref[r] = mixed.astype(jnp.bfloat16)
        return 0

    lax.fori_loop(0, REQ // 2, pair, 0)


def page_array(count):
    return jax.ShapeDtypeStruct((count, PAGE, WIDE), jnp.bfloat16)


def attend(page_table, lengths, queries, fresh, kv_cache):
    return pl.pallas_call(
        attend_kernel,
        out_shape=jax.ShapeDtypeStruct((REQ, 2 * HEADS, HD), jnp.bfloat16),
        in_specs=[SMEM, SMEM, VMEM, VMEM, VMEM],
        out_specs=VMEM,
        scratch_shapes=[pltpu.VMEM((2, CTX, WIDE), jnp.bfloat16)],
        compiler_params=pltpu.CompilerParams(vmem_limit_bytes=24 << 20),
        cost_estimate=LIGHT,
        name="attend",
    )(page_table, lengths, queries, fresh, kv_cache)


def swap(block):
    count = lax.axis_size("inst")
    return lax.ppermute(block, "inst", [(i, (i + count // 2) % count) for i in range(count)])


def in_vmem(count):
    return pltpu.VMEM((count, PAGE, WIDE), jnp.bfloat16)


def keep(*arrays):
    return [pltpu.with_memory_space_constraint(array, pltpu.VMEM) for array in arrays]


def to_neighbour(block):
    return lax.ppermute(block, "inst", [(i, i ^ GROUP) for i in range(lax.axis_size("inst"))])


def after(done, *arrays):
    return lax.optimization_barrier((done, *arrays))[1:]


def local(x_first, x_second, w_kv, q_first, q_second, kv_cache, page_table, lengths, mig_req):
    moving = mig_req.T
    first = pl.pallas_call(
        pack_first_kernel,
        out_shape=in_vmem(FIRST),
        in_specs=[SMEM, SMEM, SMEM, ANY],
        out_specs=VMEM,
        scratch_shapes=[pltpu.SemaphoreType.DMA],
        cost_estimate=LIGHT,
        name="pack_first",
    )(page_table, lengths, moving, kv_cache)
    got_first = swap(first)
    given, plan = pl.pallas_call(
        plan_kernel,
        out_shape=(in_vmem(MOVED), jax.ShapeDtypeStruct((2 + 8 * GROUP,), jnp.int32)),
        in_specs=[SMEM, SMEM, SMEM, ANY],
        out_specs=(VMEM, SMEM),
        scratch_shapes=[pltpu.SemaphoreType.DMA],
        cost_estimate=LIGHT,
        name="plan",
    )(*after(first, page_table), lengths, moving, kv_cache)
    hidden = jnp.concatenate(after(given, x_first, x_second), 0)
    share = jnp.dot(hidden, w_kv, preferred_element_type=jnp.float32)
    shares = lax.all_to_all(share.reshape(2 * REQ, 4, WIDE), "tp", split_axis=1, concat_axis=0, tiled=False)
    fresh = jnp.sum(shares, axis=0)
    given = to_neighbour(given)
    queries = jnp.stack(
        [q_first.reshape(REQ, HEADS, HD), q_second.reshape(REQ, HEADS, HD)], axis=1
    ).reshape(REQ, 2 * HEADS, HD)
    mixed = attend(page_table, lengths, queries, fresh, kv_cache)
    attn_first = mixed[:, :HEADS].reshape(REQ, HEADS * HD)
    attn_second = mixed[:, HEADS:].reshape(REQ, HEADS * HD)
    second, last = pl.pallas_call(
        pack_rest_kernel,
        out_shape=(in_vmem(HEAD + MOVED), in_vmem(REST)),
        in_specs=[SMEM, SMEM, SMEM, SMEM, VMEM, VMEM, ANY],
        out_specs=(VMEM, VMEM),
        scratch_shapes=[pltpu.SemaphoreType.DMA((2,))],
        cost_estimate=LIGHT,
        name="pack_rest",
    )(page_table, lengths, moving, *after(mixed, plan), *keep(given, fresh), kv_cache)
    blank = pl.pallas_call(
        clear_kernel,
        out_shape=page_array(SLOTS),
        in_specs=[SMEM, SMEM],
        out_specs=ANY,
        scratch_shapes=[pltpu.VMEM((MAXP, PAGE, WIDE), jnp.bfloat16), pltpu.SemaphoreType.DMA],
        cost_estimate=LIGHT,
        name="clear",
    )(lengths, *after(mixed, moving))
    choice, second, last, attn_first, attn_second, blank = lax.optimization_barrier(
        (plan[0], second, last, attn_first, attn_second, blank)
    )

    def branch(size, second, last):
        got_second = swap(second)
        got_last = swap(last[:size])
        back = to_neighbour(got_second[HEAD:])
        filler = jnp.zeros((), jnp.bfloat16)
        return got_second, back, lax.pad(got_last, filler, ((0, REST - size, 0), (0, 0, 0), (0, 0, 0)))

    got_second, back, got_last = lax.switch(
        choice, [functools.partial(branch, size) for size in SIZES], second, last
    )
    imported = pl.pallas_call(
        unpack_kernel,
        out_shape=page_array(SLOTS),
        in_specs=[SMEM, SMEM, SMEM, VMEM, VMEM, VMEM, VMEM, ANY],
        out_specs=ANY,
        scratch_shapes=[
            pltpu.VMEM((2 * REQ, WIDE), jnp.float32),
            pltpu.VMEM((MIG, 2, PAGE, WIDE), jnp.bfloat16),
            pltpu.SemaphoreType.DMA,
        ],
        input_output_aliases={7: 0},
        cost_estimate=LIGHT,
        name="unpack",
    )(lengths, moving, plan, *keep(got_first), got_second, got_last, back, blank)
    return attn_first, attn_second, imported.reshape(MIG, CTX, WIDE)


def solution(mesh):
    return jax.shard_map(
        local,
        mesh=mesh,
        in_specs=(
            P("inst", "tp"),
            P("inst", "tp"),
            P("tp", None),
            P("inst", "tp"),
            P("inst", "tp"),
            P("inst", None, "tp"),
            P("inst", None),
            P(),
            P(),
        ),
        out_specs=(P("inst", "tp"), P("inst", "tp"), P("inst", None, "tp")),
        check_vma=False,
    )
```

```python
import functools

import jax
import jax.numpy as jnp
from jax import lax
from jax.experimental import pallas as pl
from jax.experimental.pallas import tpu as pltpu
from jax.sharding import PartitionSpec as P

HD = 128
HEADS = 8
PAGE = 16
REQ = 16
MAXP = 32
MIG = 8
CTX = 512
WIDE = 2 * HD
SLOTS = MIG * MAXP
FIRST = 112
REST = SLOTS - FIRST
SIZES = (*range(8, 48, 8), *range(48, 112, 4), *range(112, REST + 1, 8))
SMEM = pl.BlockSpec(memory_space=pltpu.SMEM)
VMEM = pl.BlockSpec(memory_space=pltpu.VMEM)
ANY = pl.BlockSpec(memory_space=pltpu.HBM)


def requests_of(inst, mig_ref, len_ref):
    found = []
    offset = jnp.int32(MIG)
    for m in range(MIG):
        row = mig_ref[m, inst]
        length = len_ref[inst * REQ + row]
        whole = lax.shift_right_logical(length, 4)
        found.append((row, length, whole, offset))
        offset = offset + whole
    return found, offset


def wait_pages(ref, sem, count):
    for bit in range(9):
        size = 1 << bit
        if size <= ref.shape[0]:

            @pl.when((count >> bit) & 1 == 1)
            def _(size=size):
                part = ref.at[pl.ds(0, size)]
                pltpu.make_async_copy(part, part, sem).wait()


def pack_whole(found, table_ref, pool_ref, out_ref, sem, low, high, base):
    count = jnp.int32(0)
    for row, _, whole, offset in found:
        start = jnp.clip(low - offset, 0, whole)
        stop = jnp.clip(high - offset, 0, whole)

        def one(p, row=row, offset=offset):
            pltpu.make_async_copy(
                pool_ref.at[table_ref[row, p]], out_ref.at[offset + p - base], sem
            ).start()

        def four(step, _, start=start, one=one):
            for k in range(4):
                one(start + step * 4 + k)
            return 0

        def last(p, _, one=one):
            one(p)
            return 0

        fours = lax.shift_right_logical(stop - start, 2)
        lax.fori_loop(0, fours, four, 0)
        lax.fori_loop(start + fours * 4, stop, last, 0)
        count = count + stop - start
    return count


def pack_first_kernel(table_ref, len_ref, mig_ref, pool_ref, out_ref, sem):
    inst = lax.axis_index("inst")
    found, _ = requests_of(inst, mig_ref, len_ref)
    for m, (row, _, whole, _) in enumerate(found):
        pltpu.make_async_copy(pool_ref.at[table_ref[row, whole]], out_ref.at[m], sem).start()
    count = MIG + pack_whole(found, table_ref, pool_ref, out_ref, sem, MIG, FIRST, 0)
    wait_pages(out_ref, sem, count)


def pack_rest_kernel(table_ref, len_ref, mig_ref, pool_ref, out_ref, size_ref, sem):
    inst = lax.axis_index("inst")
    half = lax.axis_size("inst") // 2
    found, total = requests_of(inst, mig_ref, len_ref)
    count = pack_whole(found, table_ref, pool_ref, out_ref, sem, FIRST, SLOTS, FIRST)
    partner = lax.rem(inst + half, 2 * half)
    _, other = requests_of(partner, mig_ref, len_ref)
    most = jnp.maximum(total, other) - FIRST
    choice = jnp.int32(0)
    for size in SIZES[:-1]:
        choice = choice + jnp.where(most > size, 1, 0)
    size_ref[0] = choice
    wait_pages(out_ref, sem, count)


def copy_run(src_ref, src, dst_ref, dst, count, most, sem):
    for bit in range(most.bit_length() - 1, -1, -1):
        size = 1 << bit
        taken = (count >> (bit + 1)) << (bit + 1)

        @pl.when((count >> bit) & 1 == 1)
        def _(size=size, taken=taken):
            pltpu.make_async_copy(
                src_ref.at[pl.ds(src + taken, size)], dst_ref.at[pl.ds(dst + taken, size)], sem
            ).start()


def unpack_whole(found, got_ref, out_ref, sem, low, high, base):
    count = jnp.int32(0)
    for m, (_, _, whole, offset) in enumerate(found):
        start = jnp.clip(low - offset, 0, whole)
        stop = jnp.clip(high - offset, 0, whole)
        copy_run(got_ref, offset + start - base, out_ref, m * MAXP + start, stop - start, 31, sem)
        count = count + stop - start
    return count


def partner_requests(mig_ref, len_ref):
    half = lax.axis_size("inst") // 2
    partner = lax.rem(lax.axis_index("inst") + half, 2 * half)
    return requests_of(partner, mig_ref, len_ref)[0]


def clear_kernel(len_ref, mig_ref, out_ref, zeros, sem):
    found = partner_requests(mig_ref, len_ref)
    zeros[...] = jnp.zeros_like(zeros)
    count = jnp.int32(0)
    for m, (_, _, whole, _) in enumerate(found):
        empty = jnp.maximum(MAXP - 2 - whole, 0)
        copy_run(zeros, 0, out_ref, m * MAXP + whole + 2, empty, MAXP - 2, sem)
        count = count + empty
    wait_pages(out_ref, sem, count)


def unpack_kernel(len_ref, mig_ref, first_ref, rest_ref, fresh_ref, old_ref, out_ref, rows, made, sem):
    found = partner_requests(mig_ref, len_ref)
    count = unpack_whole(found, first_ref, out_ref, sem, MIG, FIRST, 0)
    count = count + unpack_whole(found, rest_ref, out_ref, sem, FIRST, SLOTS, FIRST)
    rows[...] = fresh_ref[...].astype(jnp.float32)
    place = lax.broadcasted_iota(jnp.int32, (PAGE, WIDE), 0)
    for m, (row, length, whole, _) in enumerate(found):
        rest = length & (PAGE - 1)
        first = rows[pl.ds(row, 1), :]
        second = rows[pl.ds(REQ + row, 1), :]
        page = jnp.where(place < rest, first_ref[m].astype(jnp.float32), 0.0)
        page = jnp.where(place == rest, first, page)
        page = jnp.where(place == rest + 1, second, page)
        made[m, 0] = page.astype(jnp.bfloat16)
        made[m, 1] = jnp.where(place == rest + 1 - PAGE, second, 0.0).astype(jnp.bfloat16)
        both = whole + 1 < MAXP

        @pl.when(both)
        def _(m=m, whole=whole):
            pltpu.make_async_copy(made.at[m], out_ref.at[pl.ds(m * MAXP + whole, 2)], sem).start()

        @pl.when(jnp.logical_not(both))
        def _(m=m, whole=whole):
            pltpu.make_async_copy(
                made.at[m, pl.ds(0, 1)], out_ref.at[pl.ds(m * MAXP + whole, 1)], sem
            ).start()

        count = count + jnp.where(both, 2, 1)
    wait_pages(out_ref, sem, count)


def attend_kernel(table_ref, len_ref, query_ref, fresh_ref, pool_ref, out_ref, tokens):
    inst = lax.axis_index("inst")
    place = lax.broadcasted_iota(jnp.int32, (PAGE, WIDE), 0)
    position = lax.broadcasted_iota(jnp.int32, (2 * HEADS, CTX), 1)
    late = jnp.where(lax.broadcasted_iota(jnp.int32, (2 * HEADS, CTX), 0) >= HEADS, 1, 0)

    def pair(step, _):
        for lane in range(2):
            r = step * 2 + lane
            length = len_ref[inst * REQ + r]
            whole = lax.shift_right_logical(length, 4)
            rest = length & (PAGE - 1)
            for p in range(MAXP):
                tokens[lane, pl.ds(p * PAGE, PAGE), :] = pool_ref[table_ref[r, p]]
            first = fresh_ref[pl.ds(r, 1), :]
            second = fresh_ref[pl.ds(REQ + r, 1), :]
            at = pl.ds(pl.multiple_of(whole * PAGE, PAGE), PAGE)
            page = tokens[lane, at, :].astype(jnp.float32)
            page = jnp.where(place == rest, first, page)
            page = jnp.where(place == rest + 1, second, page)
            tokens[lane, at, :] = page.astype(jnp.bfloat16)
            at = pl.ds(pl.multiple_of(jnp.minimum(whole + 1, MAXP - 1) * PAGE, PAGE), PAGE)
            page = tokens[lane, at, :].astype(jnp.float32)
            page = jnp.where(place == rest + 1 - PAGE, second, page)
            tokens[lane, at, :] = page.astype(jnp.bfloat16)
            scores = lax.dot_general(
                query_ref[r],
                tokens[lane, :, :HD],
                (((1,), (1,)), ((), ())),
                preferred_element_type=jnp.float32,
            ) * HD ** (-0.5)
            scores = jnp.where(position <= length + late, scores, -1e30)
            terms = jnp.exp(scores - jnp.max(scores, axis=-1, keepdims=True))
            weights = (terms / jnp.sum(terms, axis=-1, keepdims=True)).astype(jnp.bfloat16)
            mixed = jnp.dot(weights, tokens[lane, :, HD:], preferred_element_type=jnp.float32)
            out_ref[r] = mixed.astype(jnp.bfloat16)
        return 0

    lax.fori_loop(0, REQ // 2, pair, 0)


def page_array(count):
    return jax.ShapeDtypeStruct((count, PAGE, WIDE), jnp.bfloat16)


def attend(page_table, lengths, queries, fresh, kv_cache):
    return pl.pallas_call(
        attend_kernel,
        out_shape=jax.ShapeDtypeStruct((REQ, 2 * HEADS, HD), jnp.bfloat16),
        in_specs=[SMEM, SMEM, VMEM, VMEM, VMEM],
        out_specs=VMEM,
        scratch_shapes=[pltpu.VMEM((2, CTX, WIDE), jnp.bfloat16)],
        compiler_params=pltpu.CompilerParams(vmem_limit_bytes=24 << 20),
        cost_estimate=pl.CostEstimate(flops=70_000_000, bytes_accessed=40 << 20, transcendentals=130_000),
        name="attend",
    )(page_table, lengths, queries, fresh, kv_cache)


def swap(block):
    count = lax.axis_size("inst")
    return lax.ppermute(block, "inst", [(i, (i + count // 2) % count) for i in range(count)])


def local(x_first, x_second, w_kv, q_first, q_second, kv_cache, page_table, lengths, mig_req):
    moving = mig_req.T
    first = pl.pallas_call(
        pack_first_kernel,
        out_shape=pltpu.VMEM((FIRST, PAGE, WIDE), jnp.bfloat16),
        in_specs=[SMEM, SMEM, SMEM, ANY],
        out_specs=VMEM,
        scratch_shapes=[pltpu.SemaphoreType.DMA],
        name="pack_first",
    )(page_table, lengths, moving, kv_cache)
    got_first = swap(first)
    rest, choice = pl.pallas_call(
        pack_rest_kernel,
        out_shape=(pltpu.VMEM((REST, PAGE, WIDE), jnp.bfloat16), jax.ShapeDtypeStruct((1,), jnp.int32)),
        in_specs=[SMEM, SMEM, SMEM, ANY],
        out_specs=(VMEM, SMEM),
        scratch_shapes=[pltpu.SemaphoreType.DMA],
        name="pack_rest",
    )(page_table, lengths, moving, kv_cache)
    blank = pl.pallas_call(
        clear_kernel,
        out_shape=page_array(SLOTS),
        in_specs=[SMEM, SMEM],
        out_specs=ANY,
        scratch_shapes=[pltpu.VMEM((MAXP, PAGE, WIDE), jnp.bfloat16), pltpu.SemaphoreType.DMA],
        name="clear",
    )(lengths, moving)
    hidden = jnp.concatenate([x_first, x_second], 0)
    share = jnp.dot(hidden, w_kv, preferred_element_type=jnp.float32)
    shares = lax.all_to_all(share.reshape(2 * REQ, 4, WIDE), "tp", split_axis=1, concat_axis=0, tiled=False)
    fresh = jnp.sum(shares, axis=0)
    got_fresh = swap(fresh.astype(jnp.bfloat16))
    queries = jnp.stack(
        [q_first.reshape(REQ, HEADS, HD), q_second.reshape(REQ, HEADS, HD)], axis=1
    ).reshape(REQ, 2 * HEADS, HD)
    mixed = attend(page_table, lengths, queries, fresh, kv_cache)
    attn_first = mixed[:, :HEADS].reshape(REQ, HEADS * HD)
    attn_second = mixed[:, HEADS:].reshape(REQ, HEADS * HD)
    choice, rest, attn_first, attn_second, blank = lax.optimization_barrier(
        (choice, rest, attn_first, attn_second, blank)
    )

    def branch(size, rest):
        return lax.pad(swap(rest[:size]), jnp.zeros((), jnp.bfloat16), ((0, REST - size, 0), (0, 0, 0), (0, 0, 0)))

    got_rest = lax.switch(choice[0], [functools.partial(branch, size) for size in SIZES], rest)
    got_first, got_rest, got_fresh = (
        pltpu.with_memory_space_constraint(got, pltpu.VMEM) for got in (got_first, got_rest, got_fresh)
    )
    imported = pl.pallas_call(
        unpack_kernel,
        out_shape=page_array(SLOTS),
        in_specs=[SMEM, SMEM, VMEM, VMEM, VMEM, ANY],
        out_specs=ANY,
        scratch_shapes=[
            pltpu.VMEM((2 * REQ, WIDE), jnp.float32),
            pltpu.VMEM((MIG, 2, PAGE, WIDE), jnp.bfloat16),
            pltpu.SemaphoreType.DMA,
        ],
        input_output_aliases={5: 0},
        name="unpack",
    )(lengths, moving, got_first, got_rest, got_fresh, blank)
    return attn_first, attn_second, imported.reshape(MIG, CTX, WIDE)


def solution(mesh):
    return jax.shard_map(
        local,
        mesh=mesh,
        in_specs=(
            P("inst", "tp"),
            P("inst", "tp"),
            P("tp", None),
            P("inst", "tp"),
            P("inst", "tp"),
            P("inst", None, "tp"),
            P("inst", None),
            P(),
            P(),
        ),
        out_specs=(P("inst", "tp"), P("inst", "tp"), P("inst", None, "tp")),
        check_vma=False,
    )
```
